32 devices in a mesh: dm: 16 (over z, y, x), chan: 2 (over core).
Axes of the slice: x: 2, y: 2, z: 4, core: 2. Of those that a mesh axis runs over, the one named last changes fastest.
Arguments:
- phased: bfloat16 [16, 256, 2, 4096], P('dm', None, None, 'chan')
- filters: bfloat16 [32, 4096, 512], P('dm', 'chan'), may hold values from -0.375 to 0.375
- tap_blocks: int32 [32], replicated, may hold values from 1 to 4, as said below
- stretch_owner: int32 [4], replicated, may hold values from 0 to 15, as said below
Outputs:
- normalized_power: float32 [32, 64, 4096], P('dm', None, 'chan')
The draws below stay inside these ranges and needn't reach their ends.
Inputs may be any that keep to these rules, and one draw needn't show every extreme that they name: `stretch_owner`: the owners of the 4 stretches are distinct slots. `tap_blocks`: never falls from one trial to the next.
All inputs are finite; a program needn't handle non-finite values.
Results may differ from the reference program's by a relative error of at most 0.0003.
Values may be sent and summed in bfloat16 or wider, within the bound.
A program may use at most 128 MiB of HBM per device.

```python
import jax
import jax.numpy as jnp
from jax import lax

CHANS = 4096
TAPS = 256
BLOCK = 64
SAMPLES = 256
STRETCHES = 4
DOWN = 16
TRIALS = 32
SLOTS = 16
NBLOCKS = 4


def draw_phased(key, part):
    first, second = jax.random.split(key, 2)
    position = jnp.arange(CHANS, dtype=jnp.float32) / CHANS
    rough = jnp.exp(jax.random.uniform(second, (CHANS,), jnp.float32, -0.35, 0.35))
    amplitude = jnp.sqrt(10.0 ** position) * rough
    values = amplitude * jax.random.truncated_normal(first, -6.0, 6.0, (SLOTS, SAMPLES, 2, CHANS), jnp.float32)
    return values.astype(jnp.bfloat16)


def draw_tap_blocks(key, part):
    counts = jax.random.randint(key, (TRIALS,), 0, NBLOCKS)
    counts = jnp.sort(counts)
    counts = counts.at[0].set(0).at[TRIALS - 1].set(NBLOCKS - 1)
    return (counts + 1).astype(jnp.int32)


def draw_stretch_owner(key, part):
    first, second = jax.random.split(key)
    picked = jax.random.permutation(first, SLOTS - 1)[:STRETCHES]
    where_last = jax.random.randint(second, (), 0, STRETCHES)
    picked = jnp.where(jnp.arange(STRETCHES) == where_last, SLOTS - 1, picked)
    return picked.astype(jnp.int32)


def block_scale(stream_key, dims, cuts, least, high):
    level = 1.0
    for dim, shards_of in cuts:
        steps = jax.random.uniform(jax.random.fold_in(jax.random.fold_in(stream_key, 6), dim), (shards_of,), jnp.float32, least / len(cuts), high / len(cuts))
        level = level * jnp.repeat(jnp.exp(steps), dims[dim] // shards_of).reshape((-1,) + (1,) * (len(dims) - 1 - dim))
    return level


def scatter_about(own_key, shape, scale, bound, shards=(), kind=jnp.bfloat16):
    array = scale * jax.random.normal(own_key, shape, jnp.float32)
    if shards:
        array = array * block_scale(own_key, shape, shards, -0.22, 0.18)
    return jnp.clip(array, -bound, bound).astype(kind)


def setup_inputs(seed: int = 0) -> dict:
    keys = jax.random.split(jax.random.key(seed), 5)
    return {
        "phased": draw_phased(jax.random.fold_in(keys[4], 71), 0),
        "filters": scatter_about(keys[1], (TRIALS, CHANS, 2 * TAPS), TAPS ** -0.5, 0.375, ((0, 16), (1, 2))),
        "tap_blocks": draw_tap_blocks(jax.random.fold_in(keys[4], 71), 0),
        "stretch_owner": draw_stretch_owner(jax.random.fold_in(keys[4], 71), 0),
    }


epsilon = 1e-6


def reference(phased, filters, tap_blocks, stretch_owner):
    stretch_list = [lax.dynamic_index_in_dim(phased, stretch_owner[k], 0, keepdims=False) for k in range(STRETCHES)]
    signal = jnp.concatenate([jnp.zeros((TAPS, 2, CHANS), phased.dtype)] + stretch_list, axis=0).astype(jnp.float32)
    tap_index = jnp.arange(TAPS, dtype=jnp.int32)
    live = tap_index[None, :] < (tap_blocks * BLOCK)[:, None]
    live_both = jnp.concatenate([live, live], axis=1).astype(jnp.float32)
    taps_full = filters.astype(jnp.float32) * live_both[:, None, :]
    lag_index = TAPS + jnp.arange(SAMPLES, dtype=jnp.int32)[None, :] - tap_index[:, None]
    block_width = min(128, CHANS)
    outputs = []
    for k in range(STRETCHES):
        segment = signal[k * SAMPLES: k * SAMPLES + TAPS + SAMPLES]

        def per_block(index):
            first = (index * block_width).astype(jnp.int32)
            section = lax.dynamic_slice_in_dim(segment, first, block_width, axis=2)
            lagged = section[lag_index]
            real_part = lagged[:, :, 0, :]
            imag_part = lagged[:, :, 1, :]
            upper = jnp.concatenate([real_part, imag_part], axis=1)
            lower = jnp.concatenate([-imag_part, real_part], axis=1)
            toeplitz = jnp.concatenate([upper, lower], axis=0)
            tap_slab = lax.dynamic_slice_in_dim(taps_full, first, block_width, axis=1)
            filtered = jnp.einsum("twm,mnw->twn", tap_slab, toeplitz, precision=lax.Precision.HIGHEST)
            real_out = filtered[:, :, :SAMPLES]
            imag_out = filtered[:, :, SAMPLES:]
            energy = real_out * real_out + imag_out * imag_out
            return jnp.sum(energy.reshape(TRIALS, block_width, SAMPLES // DOWN, DOWN), axis=3) / DOWN

        blocks = lax.map(per_block, jnp.arange(CHANS // block_width, dtype=jnp.int32))
        outputs.append(blocks.transpose(1, 3, 0, 2).reshape(TRIALS, SAMPLES // DOWN, CHANS))
    detected = jnp.concatenate(outputs, axis=1)
    band = jnp.sum(detected, axis=2) / CHANS
    return detected / (band[:, :, None] + epsilon)
```

```python
import functools

import jax
import jax.numpy as jnp
import ml_dtypes
import numpy as np
from jax import lax
from jax.experimental import pallas as pl
from jax.experimental.pallas import tpu as pltpu
from jax.sharding import PartitionSpec as P

CHANS = 4096
TAPS = 256
BLOCK = 64
SAMPLES = 256
STRETCHES = 4
DOWN = 16
SPAN = 2 * BLOCK
NBLOCKS = TAPS // BLOCK
WIDE = 256
ROWS = 16

epsilon = 1e-06

LAST_BITS = ((2, 1, 0), (2, 0, 1), (0, 1, 2), (1, 0, 2))


def split_high_low(matrix):
    high = matrix.astype(ml_dtypes.bfloat16)
    low = (matrix - high.astype(np.float64)).astype(ml_dtypes.bfloat16)
    return high, low


def signal_transform():
    angle = 2 * np.pi * np.outer(np.arange(SPAN), np.arange(SPAN)) / SPAN
    out = np.zeros((2, SPAN, SPAN, 2))
    out[0, :, :, 0] = np.cos(angle)
    out[0, :, :, 1] = np.sin(angle)
    out[1, :, :, 0] = -np.sin(angle)
    out[1, :, :, 1] = np.cos(angle)
    return np.concatenate(split_high_low(out.reshape(2 * SPAN, 2 * SPAN)), axis=0)


def filter_transform():
    angle = 2 * np.pi * np.outer(np.arange(SPAN), np.arange(BLOCK)) / SPAN
    out = np.zeros((NBLOCKS, 2, SPAN, 2, NBLOCKS, BLOCK))
    for block in range(NBLOCKS):
        out[block, 0, :, 0, block] = np.cos(angle)
        out[block, 0, :, 1, block] = np.sin(angle)
        out[block, 1, :, 0, block] = -np.sin(angle)
        out[block, 1, :, 1, block] = np.cos(angle)
    out = out.reshape(NBLOCKS, 2 * SPAN, 2 * TAPS)
    return np.concatenate(split_high_low(out), axis=1)


def inverse_transform():
    groups = BLOCK // DOWN
    times = (np.arange(groups)[None, :] * DOWN + np.arange(DOWN)[:, None]).reshape(-1)
    angle = 2 * np.pi * np.outer(BLOCK + times, np.arange(SPAN)) / SPAN
    real = np.concatenate([np.cos(angle), -np.sin(angle)], axis=1)
    imag = np.concatenate([np.sin(angle), np.cos(angle)], axis=1)
    out = np.concatenate([real, imag], axis=0) / SPAN
    return np.concatenate(split_high_low(out), axis=0)


def dot(a, b):
    return jnp.dot(a, b, preferred_element_type=jnp.float32)


def kernel(trials, chunks, place_ref, live_ref, s0, s1, s2, s3, filters_ref, d_ref, g_ref, e_ref, out_ref, line, spec, resp, zhigh, zlow):
    rows = 2 * SAMPLES // chunks
    line[0:SPAN, :] = jnp.zeros((SPAN, WIDE), line.dtype)
    for k, source in enumerate((s0, s1, s2, s3)):
        for i in range(chunks):
            first = SPAN + k * 2 * SAMPLES + i * rows
            line[first:first + rows, :] = source[place_ref[k, i]]

    for p in range(NBLOCKS - 1):
        spec[p] = jnp.zeros((2 * SPAN, WIDE), jnp.float32)
    steps = STRETCHES * SAMPLES // BLOCK

    def forward(b, carry):
        window = line[pl.ds(pl.multiple_of(b * SPAN, SPAN), 2 * SPAN), :]
        spec[b + NBLOCKS - 1] = dot(d_ref[:2 * SPAN], window) + dot(d_ref[2 * SPAN:], window)
        return carry

    lax.fori_loop(0, steps, forward, 0)

    for t in range(trials):
        taps = filters_ref[t]
        for p in range(NBLOCKS):
            both = lax.dot_general(g_ref[p], taps, (((1,), (1,)), ((), ())), preferred_element_type=jnp.float32)
            live = (p < live_ref[t]).astype(jnp.float32)
            resp[t, p] = (both[:2 * SPAN] + both[2 * SPAN:]) * live

    groups = BLOCK // DOWN

    def outputs(pair, carry):
        powers = [[] for _ in range(trials)]
        for half in range(2):
            b = pair * 2 + half
            for c in range(SPAN // ROWS):
                re = slice(c * ROWS, (c + 1) * ROWS)
                im = slice(SPAN + c * ROWS, SPAN + (c + 1) * ROWS)
                sums = [None] * trials
                for p in range(NBLOCKS):
                    xr = spec[b + NBLOCKS - 1 - p, re, :]
                    xi = spec[b + NBLOCKS - 1 - p, im, :]
                    for t in range(trials):
                        hr = resp[t, p, re, :]
                        hi = resp[t, p, im, :]
                        zr = xr * hr - xi * hi
                        zi = xr * hi + xi * hr
                        sums[t] = (zr, zi) if p == 0 else (sums[t][0] + zr, sums[t][1] + zi)
                for t in range(trials):
                    for part, z in zip((re, im), sums[t]):
                        high = z.astype(jnp.bfloat16)
                        zhigh[half, t, part, :] = high
                        zlow[half, t, part, :] = (z - high.astype(jnp.float32)).astype(jnp.bfloat16)
            for t in range(trials):
                both = dot(e_ref[...], zhigh[half, t])
                y = both[:SPAN] + both[SPAN:] + dot(e_ref[:SPAN], zlow[half, t])
                energy = jnp.sum((y * y).reshape(SPAN // 8, 8, WIDE), axis=0)
                powers[t].append(energy[:groups] + energy[groups:])
        for t in range(trials):
            rows_out = pl.ds(pl.multiple_of(pair * 2 * groups, 2 * groups), 2 * groups)
            out_ref[t, rows_out, :] = jnp.concatenate(powers[t], axis=0) * (1.0 / DOWN)
        return carry

    lax.fori_loop(0, steps // 2, outputs, 0)


def detect(signals, filters, place, live):
    trials, chans, _ = filters.shape
    chunks, rows, _ = signals[0].shape
    times = STRETCHES * SAMPLES // DOWN
    steps = STRETCHES * SAMPLES // BLOCK
    d, g, e = signal_transform(), filter_transform(), inverse_transform()
    smem = pl.BlockSpec(memory_space=pltpu.SMEM)
    return pl.pallas_call(
        functools.partial(kernel, trials, chunks),
        grid=(chans // WIDE,),
        out_shape=jax.ShapeDtypeStruct((trials, times, chans), jnp.float32),
        in_specs=[smem, smem]
        + [pl.BlockSpec((chunks, rows, WIDE), lambda c: (0, 0, c))] * STRETCHES
        + [
            pl.BlockSpec((trials, WIDE, 2 * TAPS), lambda c: (0, c, 0)),
            pl.BlockSpec(d.shape, lambda c: (0, 0)),
            pl.BlockSpec(g.shape, lambda c: (0, 0, 0)),
            pl.BlockSpec(e.shape, lambda c: (0, 0)),
        ],
        out_specs=pl.BlockSpec((trials, times, WIDE), lambda c: (0, 0, c)),
        scratch_shapes=[
            pltpu.VMEM((SPAN + STRETCHES * 2 * SAMPLES, WIDE), jnp.bfloat16),
            pltpu.VMEM((steps + NBLOCKS - 1, 2 * SPAN, WIDE), jnp.float32),
            pltpu.VMEM((trials, NBLOCKS, 2 * SPAN, WIDE), jnp.float32),
            pltpu.VMEM((2, trials, 2 * SPAN, WIDE), jnp.bfloat16),
            pltpu.VMEM((2, trials, 2 * SPAN, WIDE), jnp.bfloat16),
        ],
        compiler_params=pltpu.CompilerParams(vmem_limit_bytes=40 * 1024 * 1024),
        cost_estimate=pl.CostEstimate(flops=30_000_000_000, bytes_accessed=16_000_000, transcendentals=0),
    )(place, live, *signals, filters, jnp.asarray(d), jnp.asarray(g), jnp.asarray(e))


def swap(value, axis, size, bit):
    return lax.ppermute(value, axis, [(i, i ^ (1 << bit)) for i in range(size)])


def body(dm, chan, phased, filters, tap_blocks, stretch_owner):
    trials, chans, _ = filters.shape
    me = lax.axis_index("dm")
    rows = 2 * SAMPLES // dm
    bits = dm.bit_length() - 1

    held = phased.reshape(dm, rows, chans)
    slots = lax.all_to_all(held, "dm", 0, 0, tiled=True)
    owned = [lax.dynamic_slice_in_dim(slots, stretch_owner[k], 1, 0) for k in range(STRETCHES)]
    orders = []
    for k in range(STRETCHES):
        low = [bit for bit in LAST_BITS[k] if bit < bits]
        orders.append(list(range(bits - 1, 2, -1)) + low)
    for s in range(bits):
        owned = [jnp.concatenate([a, swap(a, "dm", dm, orders[k][s])], axis=0) for k, a in enumerate(owned)]

    away = jnp.arange(dm, dtype=jnp.int32) ^ me
    place = jnp.stack([sum(((away >> orders[k][s]) & 1) << s for s in range(bits)) for k in range(STRETCHES)])
    live = lax.dynamic_slice_in_dim(tap_blocks, me * trials, trials)

    detected = detect(owned, filters, place, live)
    band = jnp.sum(detected, axis=2)
    for bit in range(chan.bit_length() - 1):
        band = band + swap(band, "chan", chan, bit)
    return detected / (band[:, :, None] / CHANS + epsilon)


def solution(mesh):
    in_specs = (P("dm", None, None, "chan"), P("dm", "chan", None), P(), P())
    out_specs = P("dm", None, "chan")
    run = functools.partial(body, mesh.shape["dm"], mesh.shape["chan"])
    return jax.shard_map(run, mesh=mesh, in_specs=in_specs, out_specs=out_specs, check_vma=False)
```

```python
import functools

import jax
import jax.numpy as jnp
import ml_dtypes
import numpy as np
from jax import lax
from jax.experimental import pallas as pl
from jax.experimental.pallas import tpu as pltpu
from jax.sharding import PartitionSpec as P

CHANS = 4096
TAPS = 256
BLOCK = 64
SAMPLES = 256
STRETCHES = 4
DOWN = 16
SPAN = 2 * BLOCK
NBLOCKS = TAPS // BLOCK
WIDE = 256
ROWS = 16

epsilon = 1e-06

LAST_BITS = ((2, 1, 0), (2, 0, 1), (0, 1, 2), (1, 0, 2))


def split_high_low(matrix):
    high = matrix.astype(ml_dtypes.bfloat16)
    low = (matrix - high.astype(np.float64)).astype(ml_dtypes.bfloat16)
    return high, low


def signal_transform():
    angle = 2 * np.pi * np.outer(np.arange(SPAN), np.arange(SPAN)) / SPAN
    out = np.zeros((2, SPAN, SPAN, 2))
    out[0, :, :, 0] = np.cos(angle)
    out[0, :, :, 1] = np.sin(angle)
    out[1, :, :, 0] = -np.sin(angle)
    out[1, :, :, 1] = np.cos(angle)
    return np.concatenate(split_high_low(out.reshape(2 * SPAN, 2 * SPAN)), axis=0)


def filter_transform():
    angle = 2 * np.pi * np.outer(np.arange(SPAN), np.arange(BLOCK)) / SPAN
    out = np.zeros((NBLOCKS, 2, SPAN, 2, NBLOCKS, BLOCK))
    for block in range(NBLOCKS):
        out[block, 0, :, 0, block] = np.cos(angle)
        out[block, 0, :, 1, block] = np.sin(angle)
        out[block, 1, :, 0, block] = -np.sin(angle)
        out[block, 1, :, 1, block] = np.cos(angle)
    out = out.reshape(NBLOCKS, 2 * SPAN, 2 * TAPS)
    return np.concatenate(split_high_low(out), axis=1)


def inverse_transform():
    groups = BLOCK // DOWN
    times = (np.arange(groups)[None, :] * DOWN + np.arange(DOWN)[:, None]).reshape(-1)
    angle = 2 * np.pi * np.outer(BLOCK + times, np.arange(SPAN)) / SPAN
    real = np.concatenate([np.cos(angle), -np.sin(angle)], axis=1)
    imag = np.concatenate([np.sin(angle), np.cos(angle)], axis=1)
    out = np.concatenate([real, imag], axis=0) / SPAN
    return np.concatenate(split_high_low(out), axis=0)


def dot(a, b):
    return jnp.dot(a, b, preferred_element_type=jnp.float32)


def kernel(trials, chunks, place_ref, live_ref, s0, s1, s2, s3, filters_ref, d_ref, g_ref, e_ref, out_ref, line, spec, resp, zhigh, zlow):
    rows = 2 * SAMPLES // chunks
    line[0:SPAN, :] = jnp.zeros((SPAN, WIDE), line.dtype)
    for k, source in enumerate((s0, s1, s2, s3)):
        for i in range(chunks):
            first = SPAN + k * 2 * SAMPLES + i * rows
            line[first:first + rows, :] = source[place_ref[k, i]]

    for p in range(NBLOCKS - 1):
        spec[p] = jnp.zeros((2 * SPAN, WIDE), jnp.float32)
    steps = STRETCHES * SAMPLES // BLOCK

    def forward(b, carry):
        window = line[pl.ds(pl.multiple_of(b * SPAN, SPAN), 2 * SPAN), :]
        spec[b + NBLOCKS - 1] = dot(d_ref[:2 * SPAN], window) + dot(d_ref[2 * SPAN:], window)
        return carry

    lax.fori_loop(0, steps, forward, 0, unroll=4)

    for t in range(trials):
        taps = filters_ref[t]
        for p in range(NBLOCKS):
            both = lax.dot_general(g_ref[p], taps, (((1,), (1,)), ((), ())), preferred_element_type=jnp.float32)
            live = (p < live_ref[t]).astype(jnp.float32)
            resp[t, p] = (both[:2 * SPAN] + both[2 * SPAN:]) * live

    groups = BLOCK // DOWN

    def outputs(pair, carry):
        powers = [[] for _ in range(trials)]
        for half in range(2):
            b = pair * 2 + half
            for c in range(SPAN // ROWS):
                re = slice(c * ROWS, (c + 1) * ROWS)
                im = slice(SPAN + c * ROWS, SPAN + (c + 1) * ROWS)
                sums = [None] * trials
                for p in range(NBLOCKS):
                    xr = spec[b + NBLOCKS - 1 - p, re, :]
                    xi = spec[b + NBLOCKS - 1 - p, im, :]
                    for t in range(trials):
                        hr = resp[t, p, re, :]
                        hi = resp[t, p, im, :]
                        zr = xr * hr - xi * hi
                        zi = xr * hi + xi * hr
                        sums[t] = (zr, zi) if p == 0 else (sums[t][0] + zr, sums[t][1] + zi)
                for t in range(trials):
                    for part, z in zip((re, im), sums[t]):
                        high = z.astype(jnp.bfloat16)
                        zhigh[half, t, part, :] = high
                        zlow[half, t, part, :] = (z - high.astype(jnp.float32)).astype(jnp.bfloat16)
            for t in range(trials):
                both = dot(e_ref[...], zhigh[half, t])
                y = both[:SPAN] + both[SPAN:] + dot(e_ref[:SPAN], zlow[half, t])
                energy = jnp.sum((y * y).reshape(SPAN // 8, 8, WIDE), axis=0)
                powers[t].append(energy[:groups] + energy[groups:])
        for t in range(trials):
            rows_out = pl.ds(pl.multiple_of(pair * 2 * groups, 2 * groups), 2 * groups)
            out_ref[t, rows_out, :] = jnp.concatenate(powers[t], axis=0) * (1.0 / DOWN)
        return carry

    lax.fori_loop(0, steps // 2, outputs, 0)


def detect(signals, filters, place, live):
    trials, chans, _ = filters.shape
    chunks, rows, _ = signals[0].shape
    times = STRETCHES * SAMPLES // DOWN
    steps = STRETCHES * SAMPLES // BLOCK
    d, g, e = signal_transform(), filter_transform(), inverse_transform()
    smem = pl.BlockSpec(memory_space=pltpu.SMEM)
    return pl.pallas_call(
        functools.partial(kernel, trials, chunks),
        grid=(chans // WIDE,),
        out_shape=jax.ShapeDtypeStruct((trials, times, chans), jnp.float32),
        in_specs=[smem, smem]
        + [pl.BlockSpec((chunks, rows, WIDE), lambda c: (0, 0, c))] * STRETCHES
        + [
            pl.BlockSpec((trials, WIDE, 2 * TAPS), lambda c: (0, c, 0)),
            pl.BlockSpec(d.shape, lambda c: (0, 0)),
            pl.BlockSpec(g.shape, lambda c: (0, 0, 0)),
            pl.BlockSpec(e.shape, lambda c: (0, 0)),
        ],
        out_specs=pl.BlockSpec((trials, times, WIDE), lambda c: (0, 0, c)),
        scratch_shapes=[
            pltpu.VMEM((SPAN + STRETCHES * 2 * SAMPLES, WIDE), jnp.bfloat16),
            pltpu.VMEM((steps + NBLOCKS - 1, 2 * SPAN, WIDE), jnp.float32),
            pltpu.VMEM((trials, NBLOCKS, 2 * SPAN, WIDE), jnp.float32),
            pltpu.VMEM((2, trials, 2 * SPAN, WIDE), jnp.bfloat16),
            pltpu.VMEM((2, trials, 2 * SPAN, WIDE), jnp.bfloat16),
        ],
        compiler_params=pltpu.CompilerParams(vmem_limit_bytes=40 * 1024 * 1024),
        cost_estimate=pl.CostEstimate(flops=30_000_000_000, bytes_accessed=16_000_000, transcendentals=0),
    )(place, live, *signals, filters, jnp.asarray(d), jnp.asarray(g), jnp.asarray(e))


def swap(value, axis, size, bit):
    return lax.ppermute(value, axis, [(i, i ^ (1 << bit)) for i in range(size)])


def body(dm, chan, phased, filters, tap_blocks, stretch_owner):
    trials, chans, _ = filters.shape
    me = lax.axis_index("dm")
    rows = 2 * SAMPLES // dm
    bits = dm.bit_length() - 1

    held = phased.reshape(dm, rows, chans)
    slots = lax.all_to_all(held, "dm", 0, 0, tiled=True)
    owned = [lax.dynamic_slice_in_dim(slots, stretch_owner[k], 1, 0) for k in range(STRETCHES)]
    orders = []
    for k in range(STRETCHES):
        low = [bit for bit in LAST_BITS[k] if bit < bits]
        orders.append(list(range(bits - 1, 2, -1)) + low)
    for s in range(bits):
        owned = [jnp.concatenate([a, swap(a, "dm", dm, orders[k][s])], axis=0) for k, a in enumerate(owned)]

    away = jnp.arange(dm, dtype=jnp.int32) ^ me
    place = jnp.stack([sum(((away >> orders[k][s]) & 1) << s for s in range(bits)) for k in range(STRETCHES)])
    live = lax.dynamic_slice_in_dim(tap_blocks, me * trials, trials)

    detected = detect(owned, filters, place, live)
    band = jnp.sum(detected, axis=2)
    for bit in range(chan.bit_length() - 1):
        band = band + swap(band, "chan", chan, bit)
    return detected / (band[:, :, None] / CHANS + epsilon)


def solution(mesh):
    in_specs = (P("dm", None, None, "chan"), P("dm", "chan", None), P(), P())
    out_specs = P("dm", None, "chan")
    run = functools.partial(body, mesh.shape["dm"], mesh.shape["chan"])
    return jax.shard_map(run, mesh=mesh, in_specs=in_specs, out_specs=out_specs, check_vma=False)
```
